256 devices in a mesh: pair: 8 (over y_hi, x), row: 32 (over y_lo, z, core).
Axes of the slice: x: 4, y: 4 (y_hi: 2, y_lo: 2; y = y_hi * 2 + y_lo), z: 8, core: 2. Of those that a mesh axis runs over, the one named last changes fastest.
Arguments:
- snapshots: float32 [65536, 2048], P('row', 'pair'), may hold values from -13 to 13
Outputs:
- rotated: float32 [65536, 2048], P('row', 'pair')
The draws below stay inside these ranges and needn't reach their ends.
All inputs are finite; a program needn't handle non-finite values.
Results may differ from the reference program's by a relative error of at most 0.0003.
Values sent between devices are 32-bit elements; how exact they have to be, the bound alone decides.
A program may use at most 64 MiB of HBM per device.

```python
import math
import jax
import jax.numpy as jnp
from jax import lax

BW = 128
ROUNDS = 3
INNER = 2
BLOCKS = 16
NCOL = 2048
ROWS = 65536


def draw_snapshots(key, part):
    key = jax.random.fold_in(key, 11)
    key_noise, key_common, key_scale = jax.random.split(key, 3)
    noise = jnp.clip(jax.random.normal(key_noise, (ROWS, NCOL), jnp.float32), -5.0, 5.0)
    common = jnp.clip(jax.random.normal(key_common, (ROWS, 1), jnp.float32), -5.0, 5.0)
    weight = 0.3
    column_scale = jnp.exp(jax.random.uniform(key_scale, (1, NCOL), jnp.float32, 0.0, math.log(2.0)))
    return column_scale * (noise + weight * common)


def setup_inputs(seed: int = 0) -> dict:
    splits = jax.random.split(jax.random.key(seed), 2)
    return {
        "snapshots": draw_snapshots(jax.random.fold_in(splits[1], 71), 0),
    }


highest = lax.Precision.HIGHEST

def eigen_rotation(gram_full):
    extent = gram_full.shape[0]
    rotation = jnp.eye(extent, dtype=gram_full.dtype)
    for repeat in range(INNER):
        images = jnp.dot(gram_full, rotation, precision=highest)
        crossed = jnp.einsum('ki,kj->ij', images, images, precision=highest)
        factor = jnp.linalg.cholesky(crossed)
        rotation = lax.linalg.triangular_solve(factor, images, left_side=False, lower=True, transpose_a=True)
    return rotation

def reference(snapshots):
    row_count = snapshots.shape[0]
    pair_count = BLOCKS // 2
    slot_blocks = snapshots.reshape(row_count, BLOCKS, BW)
    for round_index in range(ROUNDS):
        top_blocks = slot_blocks[:, 0::2, :]
        low_blocks = slot_blocks[:, 1::2, :]
        joined = jnp.concatenate([top_blocks, low_blocks], axis=2)
        grams = jnp.einsum('mpi,mpj->pij', joined, joined, precision=highest)
        rotations = jax.vmap(eigen_rotation)(grams)
        turned = jnp.einsum('mpi,pij->mpj', joined, rotations, precision=highest)
        new_top = turned[:, :, :BW]
        new_low = turned[:, :, BW:]
        moved_top = jnp.concatenate([new_top[:, :1], new_low[:, :1], new_top[:, 1:pair_count - 1]], axis=1)
        moved_low = jnp.concatenate([new_low[:, 1:], new_top[:, pair_count - 1:]], axis=1)
        slot_blocks = jnp.stack([moved_top, moved_low], axis=2).reshape(row_count, BLOCKS, BW)
    return slot_blocks.reshape(row_count, NCOL)
```

```python
import functools

import jax
import jax.numpy as jnp
from jax import lax
from jax.experimental import pallas as pl
from jax.experimental.pallas import tpu as pltpu
from jax.sharding import PartitionSpec as P

ROUNDS = 3
BW = 128
N = 2 * BW
NB = 16
STEP = 256
MESH = pl.DeviceIdType.MESH
HIGHEST = lax.Precision.HIGHEST
VMEM = pl.BlockSpec(memory_space=pltpu.VMEM)


def product(a, b, a_dim, b_dim):
    dims = (((a_dim,), (b_dim,)), ((), ()))
    return lax.dot_general(a, b, dims, precision=HIGHEST, preferred_element_type=jnp.float32)


def eliminate(block, halves):
    extent = block.shape[0]
    rows = lax.broadcasted_iota(jnp.int32, (extent, BW), 0)
    columns = [jnp.broadcast_to(block[:, i : i + 1], (extent, BW)) for i in range(extent)]
    pivots = jnp.zeros((extent, BW), jnp.float32)
    for i in range(extent):
        pivot = columns[i][i : i + 1, :]
        pivots = jnp.where(rows == i, pivot, pivots)
        if i < extent - 1:
            factor = columns[i] * (1.0 / pivot)
            for j in range(i + 1, extent):
                columns[j] = columns[j] - factor * columns[i][j : j + 1, :]
            below = jnp.where(rows > i, factor, 0.0)
            halves = [half - below * half[i : i + 1, :] for half in halves]
        yield None
    scale = lax.rsqrt(pivots)
    yield [half * scale for half in halves]


def side_by_side(chains):
    results = [None] * len(chains)
    for step in range(NB + 1):
        for index, chain in enumerate(chains):
            results[index] = next(chain)
    return results


def solve_kernel(gram_ref, basis_ref, rest_ref):
    gram = gram_ref[...]
    rest_ref[...] = product(gram, gram, 1, 0)
    panels = N // NB
    waiting = None
    for panel in range(panels + 1):
        chains = []
        start = panel * NB
        first = BW if start >= BW else 0
        if panel < panels:
            strip = rest_ref[start : start + NB, first:]
            block = strip[:, start - first : start - first + NB]
            chains.append(eliminate(block, [strip[:, c : c + BW] for c in range(0, N - first, BW)]))
        if waiting is not None:
            done = start - NB
            strip = waiting
            if done > 0:
                earlier = basis_ref[:done, :]
                strip = strip - product(product(strip, earlier, 1, 1), earlier, 1, 0)
            block = product(strip, strip, 1, 1)
            chains.append(eliminate(block, [strip[:, :BW], strip[:, BW:]]))
        results = side_by_side(chains)
        if waiting is not None:
            basis_ref[done:start, :] = jnp.concatenate(results[-1], axis=1)
        if panel < panels:
            strip = jnp.concatenate(results[0], axis=1) if first == 0 else results[0][0]
            after = start + NB
            for low, high in ((after, after + NB), (after + NB, N)):
                if low < min(high, N):
                    rest_ref[low:high, first:] -= product(strip[:, low - first : high - first], strip, 0, 0)
            row = lax.broadcasted_iota(jnp.int32, strip.shape, 0) + start
            column = lax.broadcasted_iota(jnp.int32, strip.shape, 1) + first
            strip = jnp.where(column >= row, strip, 0.0)
            waiting = strip if first == 0 else jnp.concatenate([jnp.zeros_like(strip), strip], axis=1)


def pair_solve(gram):
    return pl.pallas_call(
        solve_kernel,
        out_shape=jax.ShapeDtypeStruct((N, N), jnp.float32),
        in_specs=[VMEM],
        out_specs=VMEM,
        scratch_shapes=[pltpu.VMEM((N, N), jnp.float32)],
        compiler_params=pltpu.CompilerParams(vmem_limit_bytes=16 * 2**20),
        name="pair_solve",
    )(gram)


def places():
    pair, row = lax.axis_index("pair"), lax.axis_index("row")
    return pair, row, lax.rem(row, 2), lax.div(row, 2)


def greet(pairs, chips, with_rows, with_pairs):
    pair, row, core, chip = places()
    barrier = pltpu.get_barrier_semaphore()
    if with_rows:
        pl.semaphore_signal(barrier, inc=1, device_id=(pair, row + 1 - 2 * core), device_id_type=MESH)

        @pl.loop(1, chips)
        def _(step):
            other = lax.rem(chip + step, chips) * 2 + core
            pl.semaphore_signal(barrier, inc=1, device_id=(pair, other), device_id_type=MESH)

    if with_pairs:

        @pl.when(pair > 0)
        def _():
            pl.semaphore_signal(barrier, inc=1, device_id=(pair - 1, row), device_id_type=MESH)

        @pl.when(pair < pairs - 1)
        def _():
            pl.semaphore_signal(barrier, inc=1, device_id=(pair + 1, row), device_id_type=MESH)

    peers = chips if with_rows else 0
    if with_pairs:
        peers = peers + jnp.where(pair > 0, 1, 0) + jnp.where(pair < pairs - 1, 1, 0)
    pl.semaphore_wait(barrier, peers)


def sum_rows(chips, part_ref, total_ref, half_ref, slots_ref, sems):
    pair, row, core, chip = places()
    piece = BW // chips
    mine = pl.multiple_of(core * BW, BW)
    theirs = pl.multiple_of(BW - core * BW, BW)
    twin = (pair, row + 1 - 2 * core)

    swap = pltpu.make_async_remote_copy(
        src_ref=part_ref.at[pl.ds(theirs, BW)], dst_ref=half_ref,
        send_sem=sems.at[0], recv_sem=sems.at[1], device_id=twin, device_id_type=MESH)
    swap.start()
    swap.wait()
    half_ref[...] += part_ref[pl.ds(mine, BW), :]

    def spread(step):
        to = lax.rem(chip + step, chips)
        return pltpu.make_async_remote_copy(
            src_ref=half_ref.at[pl.ds(pl.multiple_of(to * piece, piece), piece)], dst_ref=slots_ref.at[step - 1],
            send_sem=sems.at[2], recv_sem=sems.at[3], device_id=(pair, to * 2 + core), device_id_type=MESH)

    @pl.loop(1, chips)
    def _(step):
        spread(step).start()

    place = pl.multiple_of(chip * piece, piece)
    total = half_ref[pl.ds(place, piece), :]
    everything = slots_ref.at[pl.ds(0, chips - 1)]
    pltpu.make_async_copy(everything, everything, sems.at[3]).wait()
    total_ref[pl.ds(mine + place, piece), :] = total + jnp.sum(slots_ref[...], axis=0)
    pltpu.make_async_copy(everything, everything, sems.at[2]).wait()

    @pl.loop(1, chips)
    def _(step):
        to = lax.rem(chip + step, chips)
        here = total_ref.at[pl.ds(pl.multiple_of(mine + place, piece), piece)]
        pltpu.make_async_remote_copy(
            src_ref=here, dst_ref=here,
            send_sem=sems.at[4], recv_sem=sems.at[5], device_id=(pair, to * 2 + core), device_id_type=MESH).start()

    pltpu.make_async_copy(everything, everything, sems.at[5]).wait()
    pltpu.make_async_copy(everything, everything, sems.at[4]).wait()
    swap = pltpu.make_async_remote_copy(
        src_ref=total_ref.at[pl.ds(mine, BW)], dst_ref=total_ref.at[pl.ds(mine, BW)],
        send_sem=sems.at[6], recv_sem=sems.at[7], device_id=twin, device_id_type=MESH)
    swap.start()
    swap.wait()


def gram_kernel(chips, x_ref, total_ref, part_ref, half_ref, slots_ref, sems):
    greet(0, chips, True, False)
    part_ref[...] = jnp.zeros_like(part_ref)

    @pl.loop(0, x_ref.shape[0] // STEP)
    def _(step):
        block = x_ref[pl.ds(pl.multiple_of(step * STEP, STEP), STEP), :]
        part_ref[...] += product(block, block, 0, 0)

    sum_rows(chips, part_ref, total_ref, half_ref, slots_ref, sems)


def turn_kernel(pairs, chips, with_gram, x_ref, basis_ref, *refs):
    if with_gram:
        out_ref, total_ref, turn_ref, right_ref, left_ref, pair_sems, part_ref, half_ref, slots_ref, sems = refs
    else:
        out_ref, turn_ref, right_ref, left_ref, pair_sems = refs
    pair, row, _, _ = places()
    pieces = x_ref.shape[0] // STEP
    greet(pairs, chips, with_gram, True)
    turn_ref[...] = basis_ref[...].T

    def window(step):
        return pl.ds(pl.multiple_of(step * STEP, STEP), STEP)

    def to_right(step):
        return pltpu.make_async_remote_copy(
            src_ref=right_ref.at[window(step)], dst_ref=out_ref.at[window(step), pl.ds(0, BW)],
            send_sem=pair_sems.at[0, step], recv_sem=pair_sems.at[1, step],
            device_id=(pair + 1, row), device_id_type=MESH)

    def to_left(step):
        return pltpu.make_async_remote_copy(
            src_ref=left_ref.at[window(step)], dst_ref=out_ref.at[window(step), pl.ds(BW, BW)],
            send_sem=pair_sems.at[2, step], recv_sem=pair_sems.at[3, step],
            device_id=(pair - 1, row), device_id_type=MESH)

    @pl.loop(0, pieces)
    def _(step):
        turned = product(x_ref[window(step), :], turn_ref[...], 1, 0)
        top, low = turned[:, :BW], turned[:, BW:]
        left_ref[window(step), :] = low

        @pl.when(pair == 0)
        def _():
            right_ref[window(step), :] = low
            out_ref[window(step), pl.ds(0, BW)] = top

        @pl.when(pair > 0)
        def _():
            right_ref[window(step), :] = top
            to_left(step).start()

        @pl.when(pair == pairs - 1)
        def _():
            out_ref[window(step), pl.ds(BW, BW)] = top

        @pl.when(pair < pairs - 1)
        def _():
            to_right(step).start()

    if with_gram:
        part_ref[...] = jnp.zeros_like(part_ref)

    @pl.loop(0, pieces)
    def _(step):
        @pl.when(pair > 0)
        def _():
            to_right(step).wait_recv()

        @pl.when(pair < pairs - 1)
        def _():
            to_left(step).wait_recv()

        if with_gram:
            block = out_ref[window(step), :]
            part_ref[...] += product(block, block, 0, 0)

    if with_gram:
        sum_rows(chips, part_ref, total_ref, half_ref, slots_ref, sems)

    @pl.loop(0, pieces)
    def _(step):
        @pl.when(pair > 0)
        def _():
            to_left(step).wait_send()

        @pl.when(pair < pairs - 1)
        def _():
            to_right(step).wait_send()


def sum_scratch(chips):
    return [
        pltpu.VMEM((N, N), jnp.float32),
        pltpu.VMEM((BW, N), jnp.float32),
        pltpu.VMEM((chips - 1, BW // chips, N), jnp.float32),
        pltpu.SemaphoreType.DMA((8,)),
    ]


def params(collective_id):
    return pltpu.CompilerParams(
        collective_id=collective_id, has_side_effects=True, vmem_limit_bytes=24 * 2**20
    )


def gram_sum(x, chips):
    return pl.pallas_call(
        functools.partial(gram_kernel, chips),
        out_shape=jax.ShapeDtypeStruct((N, N), jnp.float32),
        in_specs=[VMEM],
        out_specs=VMEM,
        scratch_shapes=sum_scratch(chips),
        compiler_params=params(0),
        name="gram_sum",
    )(x)


def turn(x, basis, pairs, chips, with_gram):
    rows = x.shape[0]
    scratch = [
        pltpu.VMEM((N, N), jnp.float32),
        pltpu.VMEM((rows, BW), jnp.float32),
        pltpu.VMEM((rows, BW), jnp.float32),
        pltpu.SemaphoreType.DMA((4, rows // STEP)),
    ]
    shapes = [jax.ShapeDtypeStruct(x.shape, jnp.float32)]
    if with_gram:
        scratch += sum_scratch(chips)
        shapes.append(jax.ShapeDtypeStruct((N, N), jnp.float32))
    return pl.pallas_call(
        functools.partial(turn_kernel, pairs, chips, with_gram),
        out_shape=shapes,
        in_specs=[VMEM, VMEM],
        out_specs=[VMEM] * len(shapes),
        scratch_shapes=scratch,
        compiler_params=params(1 if with_gram else 2),
        name="turn_gram" if with_gram else "turn",
    )(x, basis)


def body(pairs, chips, x):
    gram = gram_sum(x, chips)
    for round_index in range(ROUNDS - 1):
        x, gram = turn(x, pair_solve(gram), pairs, chips, True)
    return turn(x, pair_solve(gram), pairs, chips, False)[0]


def solution(mesh):
    return jax.shard_map(
        functools.partial(body, mesh.shape["pair"], mesh.shape["row"] // 2),
        mesh=mesh,
        in_specs=(P("row", "pair"),),
        out_specs=P("row", "pair"),
        check_vma=False,
    )
```

```python
import functools

import jax
import jax.numpy as jnp
from jax import lax
from jax.experimental import pallas as pl
from jax.experimental.pallas import tpu as pltpu
from jax.sharding import PartitionSpec as P

ROUNDS = 3
BW = 128
N = 2 * BW
NB = 16
STEP = 256
MESH = pl.DeviceIdType.MESH
HIGHEST = lax.Precision.HIGHEST
VMEM = pl.BlockSpec(memory_space=pltpu.VMEM)


def product(a, b, a_dim, b_dim):
    dims = (((a_dim,), (b_dim,)), ((), ()))
    return lax.dot_general(a, b, dims, precision=HIGHEST, preferred_element_type=jnp.float32)


def eliminate(block, halves):
    extent = block.shape[0]
    rows = lax.broadcasted_iota(jnp.int32, (extent, BW), 0)
    columns = [jnp.broadcast_to(block[:, i : i + 1], (extent, BW)) for i in range(extent)]
    pivots = jnp.zeros((extent, BW), jnp.float32)
    for i in range(extent):
        pivot = columns[i][i : i + 1, :]
        pivots = jnp.where(rows == i, pivot, pivots)
        if i < extent - 1:
            factor = columns[i] * (1.0 / pivot)
            for j in range(i + 1, extent):
                columns[j] = columns[j] - factor * columns[i][j : j + 1, :]
            below = jnp.where(rows > i, factor, 0.0)
            halves = [half - below * half[i : i + 1, :] for half in halves]
        yield None
    scale = lax.rsqrt(pivots)
    yield [half * scale for half in halves]


def side_by_side(chains):
    results = [None] * len(chains)
    for step in range(NB + 1):
        for index, chain in enumerate(chains):
            results[index] = next(chain)
    return results


def solve(gram_ref, basis_ref, rest_ref):
    gram = gram_ref[...]
    rest_ref[...] = product(gram, gram, 1, 0)
    panels = N // NB
    waiting = None
    for panel in range(panels + 1):
        chains = []
        start = panel * NB
        first = BW if start >= BW else 0
        if panel < panels:
            strip = rest_ref[start : start + NB, first:]
            block = strip[:, start - first : start - first + NB]
            chains.append(eliminate(block, [strip[:, c : c + BW] for c in range(0, N - first, BW)]))
        if waiting is not None:
            done = start - NB
            strip = waiting
            if done > 0:
                earlier = basis_ref[:done, :]
                strip = strip - product(product(strip, earlier, 1, 1), earlier, 1, 0)
            block = product(strip, strip, 1, 1)
            chains.append(eliminate(block, [strip[:, :BW], strip[:, BW:]]))
        results = side_by_side(chains)
        if waiting is not None:
            basis_ref[done:start, :] = jnp.concatenate(results[-1], axis=1)
        if panel < panels:
            strip = jnp.concatenate(results[0], axis=1) if first == 0 else results[0][0]
            after = start + NB
            for low, high in ((after, after + NB), (after + NB, N)):
                if low < min(high, N):
                    rest_ref[low:high, first:] -= product(strip[:, low - first : high - first], strip, 0, 0)
            row = lax.broadcasted_iota(jnp.int32, strip.shape, 0) + start
            column = lax.broadcasted_iota(jnp.int32, strip.shape, 1) + first
            strip = jnp.where(column >= row, strip, 0.0)
            waiting = strip if first == 0 else jnp.concatenate([jnp.zeros_like(strip), strip], axis=1)


def places(chips):
    pair, row = lax.axis_index("pair"), lax.axis_index("row")
    depth = chips // 2
    chip = lax.div(row, 2)
    return pair, row, lax.rem(row, 2), lax.div(chip, depth), lax.rem(chip, depth)


def greet(pairs, chips):
    pair, row, core, _, _ = places(chips)
    chip = lax.div(row, 2)
    barrier = pltpu.get_barrier_semaphore()

    def call(to_pair, to_row):
        pl.semaphore_signal(barrier, inc=1, device_id=(to_pair, to_row), device_id_type=MESH)

    @pl.when(pair > 0)
    def _():
        call(pair - 1, row)

    @pl.when(pair < pairs - 1)
    def _():
        call(pair + 1, row)

    for flip in (1, 2, 3):
        call(pair, quad_row(chips, flip))

    @pl.loop(1, chips)
    def _(step):
        @pl.when(step != chips // 2)
        def _():
            call(pair, lax.rem(chip + step, chips) * 2 + core)

    neighbours = jnp.where(pair > 0, 1, 0) + jnp.where(pair < pairs - 1, 1, 0)
    return lambda: pl.semaphore_wait(barrier, neighbours + 3 + chips - 2)


def quad_row(chips, flip):
    _, _, core, y, z = places(chips)
    to_core = 1 - core if flip & 1 else core
    to_y = 1 - y if flip & 2 else y
    return (to_y * (chips // 2) + z) * 2 + to_core


def copy_to(src, dst, send_sem, recv_sem, pair, row):
    return pltpu.make_async_remote_copy(
        src_ref=src, dst_ref=dst, send_sem=send_sem, recv_sem=recv_sem,
        device_id=(pair, row), device_id_type=MESH)


def wait_bytes(ref, sem):
    pltpu.make_async_copy(ref, ref, sem).wait()


def sum_all(chips, part_ref, total_ref, half_ref, slots_ref, sems):
    pair, row, core, _, _ = places(chips)
    chip = lax.div(row, 2)
    piece = BW // chips
    mine = pl.multiple_of(core * BW, BW)
    theirs = pl.multiple_of(BW - core * BW, BW)
    twin = row + 1 - 2 * core

    swap = copy_to(part_ref.at[pl.ds(theirs, BW)], half_ref, sems.at[0], sems.at[1], pair, twin)
    swap.start()
    swap.wait()
    half_ref[...] += part_ref[pl.ds(mine, BW), :]

    @pl.loop(1, chips)
    def _(step):
        to = lax.rem(chip + step, chips)
        copy_to(half_ref.at[pl.ds(pl.multiple_of(to * piece, piece), piece)], slots_ref.at[step - 1],
                sems.at[2], sems.at[3], pair, to * 2 + core).start()

    place = pl.multiple_of(chip * piece, piece)
    total = half_ref[pl.ds(place, piece), :]
    wait_bytes(slots_ref, sems.at[3])
    here = pl.ds(pl.multiple_of(mine + place, piece), piece)
    total_ref[here, :] = total + jnp.sum(slots_ref[...], axis=0)
    wait_bytes(slots_ref, sems.at[2])

    @pl.loop(1, chips)
    def _(step):
        to = lax.rem(chip + step, chips)
        copy_to(total_ref.at[here], total_ref.at[here], sems.at[4], sems.at[5], pair, to * 2 + core).start()

    wait_bytes(slots_ref, sems.at[5])
    wait_bytes(slots_ref, sems.at[4])
    swap = copy_to(total_ref.at[pl.ds(mine, BW)], total_ref.at[pl.ds(mine, BW)], sems.at[6], sems.at[7], pair, twin)
    swap.start()
    swap.wait()


def sum_cross(chips, parity, cross_ref, total_ref, near_ref, far_ref, sems):
    pair, row, core, y, z = places(chips)
    depth = chips // 2
    quarter = BW // 4

    def of(to_core, to_y):
        return pl.ds(pl.multiple_of((to_core * 2 + to_y) * quarter, quarter), quarter)

    def others(src, dst, send, recv):
        return [copy_to(src(flip), dst(flip), send.at[flip - 1], recv.at[flip - 1], pair, quad_row(chips, flip))
                for flip in (1, 2, 3)]

    def theirs(flip):
        return cross_ref.at[of(1 - core if flip & 1 else core, 1 - y if flip & 2 else y)]

    copies = others(theirs, lambda flip: near_ref.at[flip - 1], sems.at[0], sems.at[1])
    for copy in copies:
        copy.start()
    for copy in copies:
        copy.wait_recv()
    mine = far_ref.at[parity, z]
    mine[...] = (cross_ref[of(core, y), :] + near_ref[0]) + (near_ref[1] + near_ref[2])

    @pl.loop(1, depth)
    def _(step):
        to = (y * depth + lax.rem(z + step, depth)) * 2 + core
        copy_to(mine, mine, sems.at[2, parity], sems.at[3, parity], pair, to).start()

    for copy in copies:
        copy.wait_send()
    others_far = far_ref.at[parity, pl.ds(0, depth - 1)]
    wait_bytes(others_far, sems.at[3, parity])
    total_ref[of(core, y), :] = jnp.sum(far_ref[parity], axis=0)
    here = total_ref.at[of(core, y)]
    copies = others(lambda flip: here, lambda flip: here, sems.at[4], sems.at[5])
    for copy in copies:
        copy.start()
    wait_bytes(others_far, sems.at[2, parity])
    for copy in copies:
        copy.wait_recv()
    for copy in copies:
        copy.wait_send()


def rounds_kernel(pairs, chips, x_ref, out_ref, blocks_ref, gram_ref, part_ref, half_ref, slots_ref, basis_ref,
                  rest_ref, turn_ref, right_ref, left_ref, cross_ref, total_ref, near_ref, far_ref,
                  square_ref, square_in_ref, load_sem, all_sems, cross_sems, pair_sems, square_sems):
    pair, row, _, _, _ = places(chips)
    pieces = out_ref.shape[0] // STEP
    is_first, is_last = pair == 0, pair == pairs - 1

    def window(step):
        return pl.ds(pl.multiple_of(step * STEP, STEP), STEP)

    load = pltpu.make_async_copy(x_ref, blocks_ref.at[0], load_sem)
    load.start()
    arrive = greet(pairs, chips)
    part_ref[...] = jnp.zeros_like(part_ref)
    load.wait()

    @pl.loop(0, pieces)
    def _(step):
        block = blocks_ref[0, window(step), :]
        part_ref[...] += product(block, block, 0, 0)

    arrive()
    sum_all(chips, part_ref, gram_ref, half_ref, slots_ref, all_sems)

    @pl.loop(0, ROUNDS)
    def _(turn):
        parity = lax.rem(turn, 2)
        later = 1 - parity
        old, new = blocks_ref.at[parity], blocks_ref.at[later]
        solve(gram_ref, basis_ref, rest_ref)
        turn_ref[...] = basis_ref[...].T

        def to_right(step):
            return copy_to(right_ref.at[window(step)], new.at[window(step), pl.ds(0, BW)],
                           pair_sems.at[parity, 0, step], pair_sems.at[parity, 1, step], pair + 1, row)

        def to_left(step):
            return copy_to(left_ref.at[window(step)], new.at[window(step), pl.ds(BW, BW)],
                           pair_sems.at[parity, 2, step], pair_sems.at[parity, 3, step], pair - 1, row)

        def square_right():
            return copy_to(square_ref.at[0], square_in_ref.at[parity, 0],
                           square_sems.at[parity, 0], square_sems.at[parity, 1], pair + 1, row)

        def square_left():
            return copy_to(square_ref.at[1], square_in_ref.at[parity, 1],
                           square_sems.at[parity, 2], square_sems.at[parity, 3], pair - 1, row)

        @pl.loop(0, pieces)
        def _(step):
            turned = product(old[window(step), :], turn_ref[...], 1, 0)
            top, low = turned[:, :BW], turned[:, BW:]
            left_ref[window(step), :] = low

            @pl.when(is_first)
            def _():
                right_ref[window(step), :] = low
                new[window(step), pl.ds(0, BW)] = top

            @pl.when(pair > 0)
            def _():
                right_ref[window(step), :] = top
                to_left(step).start()

            @pl.when(is_last)
            def _():
                new[window(step), pl.ds(BW, BW)] = top

            @pl.when(pair < pairs - 1)
            def _():
                to_right(step).start()

        top_rows, low_rows = basis_ref[:BW, :], basis_ref[BW:, :]
        top_square = product(product(top_rows, gram_ref[...], 1, 0), top_rows, 1, 1)
        low_square = product(product(low_rows, gram_ref[...], 1, 0), low_rows, 1, 1)
        square_ref[1] = low_square

        @pl.when(is_first)
        def _():
            square_ref[0] = low_square
            square_in_ref[parity, 0] = top_square

        @pl.when(pair > 0)
        def _():
            square_ref[0] = top_square
            square_left().start()

        @pl.when(is_last)
        def _():
            square_in_ref[parity, 1] = top_square

        @pl.when(pair < pairs - 1)
        def _():
            square_right().start()

        cross_ref[...] = jnp.zeros_like(cross_ref)

        @pl.loop(0, pieces)
        def _(step):
            @pl.when(pair > 0)
            def _():
                to_right(step).wait_recv()

            @pl.when(pair < pairs - 1)
            def _():
                to_left(step).wait_recv()

            block = new[window(step), :]
            cross_ref[...] += product(block[:, :BW], block[:, BW:], 0, 0)

        @pl.when(turn < ROUNDS - 1)
        def _():
            sum_cross(chips, parity, cross_ref, total_ref, near_ref, far_ref, cross_sems)

        @pl.when(pair > 0)
        def _():
            square_right().wait_recv()
            square_left().wait_send()

        @pl.when(pair < pairs - 1)
        def _():
            square_left().wait_recv()
            square_right().wait_send()

        total = total_ref[...]
        gram_ref[:BW, :BW] = square_in_ref[parity, 0]
        gram_ref[:BW, BW:] = total
        gram_ref[BW:, :BW] = total.T
        gram_ref[BW:, BW:] = square_in_ref[parity, 1]

        @pl.loop(0, pieces)
        def _(step):
            @pl.when(pair > 0)
            def _():
                to_left(step).wait_send()

            @pl.when(pair < pairs - 1)
            def _():
                to_right(step).wait_send()

    out_ref[...] = blocks_ref[ROUNDS % 2]


def body(pairs, chips, x):
    rows = x.shape[0]
    depth, pieces = chips // 2, rows // STEP
    f32 = jnp.float32
    square = pltpu.VMEM((N, N), f32)
    tile = pltpu.VMEM((BW, BW), f32)
    dma = pltpu.SemaphoreType.DMA
    return pl.pallas_call(
        functools.partial(rounds_kernel, pairs, chips),
        out_shape=jax.ShapeDtypeStruct(x.shape, f32),
        in_specs=[pl.BlockSpec(memory_space=pl.ANY)],
        out_specs=VMEM,
        scratch_shapes=[
            pltpu.VMEM((2, rows, N), f32),
            square,
            square,
            pltpu.VMEM((BW, N), f32),
            pltpu.VMEM((chips - 1, BW // chips, N), f32),
            square,
            square,
            square,
            pltpu.VMEM((rows, BW), f32),
            pltpu.VMEM((rows, BW), f32),
            tile,
            tile,
            pltpu.VMEM((3, BW // 4, BW), f32),
            pltpu.VMEM((2, depth, BW // 4, BW), f32),
            pltpu.VMEM((2, BW, BW), f32),
            pltpu.VMEM((2, 2, BW, BW), f32),
            dma,
            dma((8,)),
            dma((6, 3)),
            dma((2, 4, pieces)),
            dma((2, 4)),
        ],
        compiler_params=pltpu.CompilerParams(
            collective_id=0, has_side_effects=True, vmem_limit_bytes=32 * 2**20
        ),
        name="rounds",
    )(x)


def solution(mesh):
    return jax.shard_map(
        functools.partial(body, mesh.shape["pair"], mesh.shape["row"] // 2),
        mesh=mesh,
        in_specs=(P("row", "pair"),),
        out_specs=P("row", "pair"),
        check_vma=False,
    )
```

```python
import functools

import jax
import jax.numpy as jnp
from jax import lax
from jax.experimental import pallas as pl
from jax.experimental.pallas import tpu as pltpu
from jax.sharding import PartitionSpec as P

ROUNDS = 3
BW = 128
N = 2 * BW
NB = 16
STEP = 128
AHEAD = 7
MARKS = (0, 1, 1)
MESH = pl.DeviceIdType.MESH
HIGHEST = lax.Precision.HIGHEST
VMEM = pl.BlockSpec(memory_space=pltpu.VMEM)


def product(a, b, a_dim, b_dim):
    dims = (((a_dim,), (b_dim,)), ((), ()))
    return lax.dot_general(a, b, dims, precision=HIGHEST, preferred_element_type=jnp.float32)


def eliminate(block, halves):
    extent = block.shape[0]
    rows = lax.broadcasted_iota(jnp.int32, (extent, BW), 0)
    columns = [jnp.broadcast_to(block[:, i : i + 1], (extent, BW)) for i in range(extent)]
    pivots = jnp.zeros((extent, BW), jnp.float32)
    for i in range(extent):
        pivot = columns[i][i : i + 1, :]
        pivots = jnp.where(rows == i, pivot, pivots)
        if i < extent - 1:
            factor = columns[i] * (1.0 / pivot)
            for j in range(i + 1, extent):
                columns[j] = columns[j] - factor * columns[i][j : j + 1, :]
            below = jnp.where(rows > i, factor, 0.0)
            halves = [half - below * half[i : i + 1, :] for half in halves]
        yield None
    scale = lax.rsqrt(pivots)
    yield [half * scale for half in halves]


def side_by_side(chains):
    results = [None] * len(chains)
    for step in range(NB + 1):
        for index, chain in enumerate(chains):
            results[index] = next(chain)
    return results


def solve(gram_ref, basis_ref, rest_ref):
    gram = gram_ref[...]
    rest_ref[...] = product(gram, gram, 1, 0)
    panels = N // NB
    waiting = None
    for panel in range(panels + 1):
        chains = []
        start = panel * NB
        first = BW if start >= BW else 0
        if panel < panels:
            strip = rest_ref[start : start + NB, first:]
            block = strip[:, start - first : start - first + NB]
            chains.append(eliminate(block, [strip[:, c : c + BW] for c in range(0, N - first, BW)]))
        if waiting is not None:
            done = start - NB
            strip = waiting
            if done > 0:
                earlier = basis_ref[:done, :]
                strip = strip - product(product(strip, earlier, 1, 1), earlier, 1, 0)
            block = product(strip, strip, 1, 1)
            chains.append(eliminate(block, [strip[:, :BW], strip[:, BW:]]))
        results = side_by_side(chains)
        if waiting is not None:
            basis_ref[done:start, :] = jnp.concatenate(results[-1], axis=1)
        if panel < panels:
            strip = jnp.concatenate(results[0], axis=1) if first == 0 else results[0][0]
            after = start + NB
            for low, high in ((after, after + NB), (after + NB, N)):
                if low < min(high, N):
                    rest_ref[low:high, first:] -= product(strip[:, low - first : high - first], strip, 0, 0)
            row = lax.broadcasted_iota(jnp.int32, strip.shape, 0) + start
            column = lax.broadcasted_iota(jnp.int32, strip.shape, 1) + first
            strip = jnp.where(column >= row, strip, 0.0)
            waiting = strip if first == 0 else jnp.concatenate([jnp.zeros_like(strip), strip], axis=1)


def places(chips):
    pair, row = lax.axis_index("pair"), lax.axis_index("row")
    depth = chips // 2
    chip = lax.div(row, 2)
    return pair, row, lax.rem(row, 2), lax.div(chip, depth), lax.rem(chip, depth)


def greet(pairs, chips):
    pair, row, core, _, _ = places(chips)
    chip = lax.div(row, 2)
    barrier = pltpu.get_barrier_semaphore()

    def call(to_pair, to_row):
        pl.semaphore_signal(barrier, inc=1, device_id=(to_pair, to_row), device_id_type=MESH)

    @pl.when(pair > 0)
    def _():
        call(pair - 1, row)

    @pl.when(pair < pairs - 1)
    def _():
        call(pair + 1, row)

    for flip in (1, 2, 3):
        call(pair, quad_row(chips, flip))

    @pl.loop(1, chips)
    def _(step):
        @pl.when(step != chips // 2)
        def _():
            call(pair, lax.rem(chip + step, chips) * 2 + core)

    neighbours = jnp.where(pair > 0, 1, 0) + jnp.where(pair < pairs - 1, 1, 0)
    return lambda: pl.semaphore_wait(barrier, neighbours + 3 + chips - 2)


def quad_row(chips, flip):
    _, _, core, y, z = places(chips)
    to_core = 1 - core if flip & 1 else core
    to_y = 1 - y if flip & 2 else y
    return (to_y * (chips // 2) + z) * 2 + to_core


def copy_to(src, dst, send_sem, recv_sem, pair, row):
    return pltpu.make_async_remote_copy(
        src_ref=src, dst_ref=dst, send_sem=send_sem, recv_sem=recv_sem,
        device_id=(pair, row), device_id_type=MESH)


def wait_bytes(ref, sem):
    pltpu.make_async_copy(ref, ref, sem).wait()


def sum_all(chips, part_ref, total_ref, half_ref, slots_ref, sems, beside):
    pair, row, core, _, _ = places(chips)
    chip = lax.div(row, 2)
    piece = BW // chips
    mine = pl.multiple_of(core * BW, BW)
    theirs = pl.multiple_of(BW - core * BW, BW)
    twin = row + 1 - 2 * core

    swap = copy_to(part_ref.at[pl.ds(theirs, BW)], half_ref, sems.at[0], sems.at[1], pair, twin)
    swap.start()
    swap.wait()
    half_ref[...] += part_ref[pl.ds(mine, BW), :]

    @pl.loop(1, chips)
    def _(step):
        to = lax.rem(chip + step, chips)
        copy_to(half_ref.at[pl.ds(pl.multiple_of(to * piece, piece), piece)], slots_ref.at[step - 1],
                sems.at[2], sems.at[3], pair, to * 2 + core).start()

    beside(0)

    place = pl.multiple_of(chip * piece, piece)
    total = half_ref[pl.ds(place, piece), :]
    wait_bytes(slots_ref, sems.at[3])
    here = pl.ds(pl.multiple_of(mine + place, piece), piece)
    total_ref[here, :] = total + jnp.sum(slots_ref[...], axis=0)
    wait_bytes(slots_ref, sems.at[2])

    @pl.loop(1, chips)
    def _(step):
        to = lax.rem(chip + step, chips)
        copy_to(total_ref.at[here], total_ref.at[here], sems.at[4], sems.at[5], pair, to * 2 + core).start()

    beside(1)

    wait_bytes(slots_ref, sems.at[5])
    wait_bytes(slots_ref, sems.at[4])
    swap = copy_to(total_ref.at[pl.ds(mine, BW)], total_ref.at[pl.ds(mine, BW)], sems.at[6], sems.at[7], pair, twin)
    swap.start()
    beside(2)
    swap.wait()


def sum_cross(chips, parity, cross_ref, total_ref, near_ref, far_ref, sems, beside):
    pair, row, core, y, z = places(chips)
    depth = chips // 2
    quarter = BW // 4

    def of(to_core, to_y):
        return pl.ds(pl.multiple_of((to_core * 2 + to_y) * quarter, quarter), quarter)

    def others(src, dst, send, recv):
        return [copy_to(src(flip), dst(flip), send.at[flip - 1], recv.at[flip - 1], pair, quad_row(chips, flip))
                for flip in (1, 2, 3)]

    def theirs(flip):
        return cross_ref.at[of(1 - core if flip & 1 else core, 1 - y if flip & 2 else y)]

    copies = others(theirs, lambda flip: near_ref.at[flip - 1], sems.at[0], sems.at[1])
    for copy in copies:
        copy.start()
    beside(0)
    for copy in copies:
        copy.wait_recv()
    mine = far_ref.at[parity, z]
    mine[...] = (cross_ref[of(core, y), :] + near_ref[0]) + (near_ref[1] + near_ref[2])

    @pl.loop(1, depth)
    def _(step):
        to = (y * depth + lax.rem(z + step, depth)) * 2 + core
        copy_to(mine, mine, sems.at[2, parity], sems.at[3, parity], pair, to).start()

    beside(1)

    for copy in copies:
        copy.wait_send()
    others_far = far_ref.at[parity, pl.ds(0, depth - 1)]
    wait_bytes(others_far, sems.at[3, parity])
    total_ref[of(core, y), :] = jnp.sum(far_ref[parity], axis=0)
    here = total_ref.at[of(core, y)]
    copies = others(lambda flip: here, lambda flip: here, sems.at[4], sems.at[5])
    for copy in copies:
        copy.start()
    beside(2)
    wait_bytes(others_far, sems.at[2, parity])
    for copy in copies:
        copy.wait_recv()
    for copy in copies:
        copy.wait_send()


def rounds_kernel(pairs, chips, x_ref, out_ref, blocks_ref, gram_ref, part_ref, half_ref, slots_ref, basis_ref,
                  rest_ref, turn_ref, right_ref, left_ref, cross_ref, total_ref, near_ref, far_ref,
                  square_ref, square_in_ref, ahead_ref, basis_in_ref, load_sem, all_sems, cross_sems, pair_sems,
                  square_sems, ahead_sems, basis_sems):
    pair, row, _, _, _ = places(chips)
    pieces = out_ref.shape[0] // STEP
    is_first, is_last = pair == 0, pair == pairs - 1

    def window(step):
        return pl.ds(pl.multiple_of(step * STEP, STEP), STEP)

    def both_ways(left, right):
        @pl.when(pair > 0)
        def _():
            left()

        @pl.when(pair < pairs - 1)
        def _():
            right()

    def ahead_right(parity, step):
        return copy_to(blocks_ref.at[parity, window(step)], ahead_ref.at[parity, 0, window(step)],
                       ahead_sems.at[parity, 0, step], ahead_sems.at[parity, 1, step], pair + 1, row)

    def ahead_left(parity, step):
        return copy_to(blocks_ref.at[parity, window(step)], ahead_ref.at[parity, 1, window(step)],
                       ahead_sems.at[parity, 2, step], ahead_sems.at[parity, 3, step], pair - 1, row)

    def send_ahead(parity, low, high):
        @pl.loop(low, high)
        def _(step):
            both_ways(lambda: ahead_left(parity, step).start(), lambda: ahead_right(parity, step).start())

    def beside(parity):
        return lambda stage: send_ahead(parity, MARKS[stage - 1] if stage else 0, MARKS[stage])

    load = pltpu.make_async_copy(x_ref, blocks_ref.at[0], load_sem)
    load.start()
    arrive = greet(pairs, chips)
    part_ref[...] = jnp.zeros_like(part_ref)
    load.wait()

    @pl.loop(0, pieces)
    def _(step):
        block = blocks_ref[0, window(step), :]
        part_ref[...] += product(block, block, 0, 0)

    arrive()
    sum_all(chips, part_ref, gram_ref, half_ref, slots_ref, all_sems, beside(0))

    @pl.loop(0, ROUNDS)
    def _(turn):
        parity = lax.rem(turn, 2)
        later = 1 - parity
        old, new = blocks_ref.at[parity], blocks_ref.at[later]

        def to_right(step):
            return copy_to(right_ref.at[window(step - AHEAD)], new.at[window(step), pl.ds(0, BW)],
                           pair_sems.at[parity, 0, step], pair_sems.at[parity, 1, step], pair + 1, row)

        def to_left(step):
            return copy_to(left_ref.at[window(step - AHEAD)], new.at[window(step), pl.ds(BW, BW)],
                           pair_sems.at[parity, 2, step], pair_sems.at[parity, 3, step], pair - 1, row)

        def square_right():
            return copy_to(square_ref.at[0], square_in_ref.at[parity, 0],
                           square_sems.at[parity, 0], square_sems.at[parity, 1], pair + 1, row)

        def square_left():
            return copy_to(square_ref.at[1], square_in_ref.at[parity, 1],
                           square_sems.at[parity, 2], square_sems.at[parity, 3], pair - 1, row)

        def basis_right():
            start = pl.multiple_of(jnp.where(is_first, BW, 0), BW)
            return copy_to(basis_ref.at[pl.ds(start, BW)], basis_in_ref.at[parity, 0],
                           basis_sems.at[parity, 0], basis_sems.at[parity, 1], pair + 1, row)

        def basis_left():
            return copy_to(basis_ref.at[pl.ds(BW, BW)], basis_in_ref.at[parity, 1],
                           basis_sems.at[parity, 2], basis_sems.at[parity, 3], pair - 1, row)

        send_ahead(parity, MARKS[2], AHEAD)
        solve(gram_ref, basis_ref, rest_ref)

        @pl.loop(0, AHEAD)
        def _(step):
            both_ways(lambda: ahead_left(parity, step).wait_send(), lambda: ahead_right(parity, step).wait_send())

        both_ways(lambda: basis_left().start(), lambda: basis_right().start())
        turn_ref[...] = basis_ref[...].T

        @pl.when(is_first | is_last)
        def _():
            @pl.loop(0, pieces)
            def _(step):
                top = product(old[window(step), :], turn_ref[:, :BW], 1, 0)

                @pl.when(is_first)
                def _():
                    new[window(step), pl.ds(0, BW)] = top

                @pl.when(is_last)
                def _():
                    new[window(step), pl.ds(BW, BW)] = top

        @pl.loop(AHEAD, pieces)
        def _(step):
            turned = product(old[window(step), :], turn_ref[...], 1, 0)
            top, low = turned[:, :BW], turned[:, BW:]
            left_ref[window(step - AHEAD), :] = low
            right_ref[window(step - AHEAD), :] = jnp.where(is_first, low, top)
            both_ways(lambda: to_left(step).start(), lambda: to_right(step).start())

        top_rows, low_rows = basis_ref[:BW, :], basis_ref[BW:, :]
        top_square = product(product(top_rows, gram_ref[...], 1, 0), top_rows, 1, 1)
        low_square = product(product(low_rows, gram_ref[...], 1, 0), low_rows, 1, 1)
        square_ref[0] = jnp.where(is_first, low_square, top_square)
        square_ref[1] = low_square
        both_ways(lambda: square_left().start(), lambda: square_right().start())

        @pl.when(is_first)
        def _():
            square_in_ref[parity, 0] = top_square

        @pl.when(is_last)
        def _():
            square_in_ref[parity, 1] = top_square

        both_ways(lambda: basis_right().wait_recv(), lambda: basis_left().wait_recv())
        cross_ref[...] = jnp.zeros_like(cross_ref)

        def add_cross(step):
            block = new[window(step), :]
            cross_ref[...] += product(block[:, :BW], block[:, BW:], 0, 0)

        @pl.when(pair > 0)
        def _():
            turn_ref[:, :BW] = basis_in_ref[parity, 0].T

        @pl.when(pair < pairs - 1)
        def _():
            turn_ref[:, BW:] = basis_in_ref[parity, 1].T

        @pl.loop(0, AHEAD)
        def _(step):
            @pl.when(pair > 0)
            def _():
                ahead_right(parity, step).wait_recv()
                new[window(step), pl.ds(0, BW)] = product(
                    ahead_ref[parity, 0, window(step), :], turn_ref[:, :BW], 1, 0)

            @pl.when(pair < pairs - 1)
            def _():
                ahead_left(parity, step).wait_recv()
                new[window(step), pl.ds(BW, BW)] = product(
                    ahead_ref[parity, 1, window(step), :], turn_ref[:, BW:], 1, 0)

            add_cross(step)

        @pl.loop(AHEAD, pieces)
        def _(step):
            both_ways(lambda: to_right(step).wait_recv(), lambda: to_left(step).wait_recv())
            add_cross(step)

        @pl.when(turn < ROUNDS - 1)
        def _():
            sum_cross(chips, parity, cross_ref, total_ref, near_ref, far_ref, cross_sems, beside(later))

        both_ways(lambda: square_right().wait_recv(), lambda: square_left().wait_recv())
        both_ways(lambda: square_left().wait_send(), lambda: square_right().wait_send())
        both_ways(lambda: basis_left().wait_send(), lambda: basis_right().wait_send())
        total = total_ref[...]
        gram_ref[:BW, :BW] = square_in_ref[parity, 0]
        gram_ref[:BW, BW:] = total
        gram_ref[BW:, :BW] = total.T
        gram_ref[BW:, BW:] = square_in_ref[parity, 1]

        @pl.loop(AHEAD, pieces)
        def _(step):
            both_ways(lambda: to_left(step).wait_send(), lambda: to_right(step).wait_send())

    out_ref[...] = blocks_ref[ROUNDS % 2]


def body(pairs, chips, x):
    rows = x.shape[0]
    depth, pieces = chips // 2, rows // STEP
    f32 = jnp.float32
    square = pltpu.VMEM((N, N), f32)
    tile = pltpu.VMEM((BW, BW), f32)
    dma = pltpu.SemaphoreType.DMA
    return pl.pallas_call(
        functools.partial(rounds_kernel, pairs, chips),
        out_shape=jax.ShapeDtypeStruct(x.shape, f32),
        in_specs=[pl.BlockSpec(memory_space=pl.ANY)],
        out_specs=VMEM,
        scratch_shapes=[
            pltpu.VMEM((2, rows, N), f32),
            square,
            square,
            pltpu.VMEM((BW, N), f32),
            pltpu.VMEM((chips - 1, BW // chips, N), f32),
            square,
            square,
            square,
            pltpu.VMEM((rows - AHEAD * STEP, BW), f32),
            pltpu.VMEM((rows - AHEAD * STEP, BW), f32),
            tile,
            tile,
            pltpu.VMEM((3, BW // 4, BW), f32),
            pltpu.VMEM((2, depth, BW // 4, BW), f32),
            pltpu.VMEM((2, BW, BW), f32),
            pltpu.VMEM((2, 2, BW, BW), f32),
            pltpu.VMEM((2, 2, AHEAD * STEP, N), f32),
            pltpu.VMEM((2, 2, BW, N), f32),
            dma,
            dma((8,)),
            dma((6, 3)),
            dma((2, 4, pieces)),
            dma((2, 4)),
            dma((2, 4, pieces)),
            dma((2, 4)),
        ],
        compiler_params=pltpu.CompilerParams(
            collective_id=0, has_side_effects=True, vmem_limit_bytes=32 * 2**20
        ),
        name="rounds",
    )(x)


def solution(mesh):
    return jax.shard_map(
        functools.partial(body, mesh.shape["pair"], mesh.shape["row"] // 2),
        mesh=mesh,
        in_specs=(P("row", "pair"),),
        out_specs=P("row", "pair"),
        check_vma=False,
    )
```

```python
import functools

import jax
import jax.numpy as jnp
from jax import lax
from jax.experimental import pallas as pl
from jax.experimental.pallas import tpu as pltpu
from jax.sharding import PartitionSpec as P

ROUNDS = 3
BW = 128
N = 2 * BW
NB = 32
INNER_NB = 16
SUB = 8
LAG = 2
STEP = 128
AHEAD = 5
MARKS = (0, 1, 1)
MESH = pl.DeviceIdType.MESH
HIGHEST = lax.Precision.HIGHEST
VMEM = pl.BlockSpec(memory_space=pltpu.VMEM)


def product(a, b, a_dim, b_dim):
    dims = (((a_dim,), (b_dim,)), ((), ()))
    return lax.dot_general(a, b, dims, precision=HIGHEST, preferred_element_type=jnp.float32)


def eliminate(block, strips):
    groups = NB // SUB
    rows = lax.broadcasted_iota(jnp.int32, (SUB, BW), 0)

    def cut(array):
        return [array[group * SUB : (group + 1) * SUB, :] for group in range(groups)]

    block, strips = cut(block), [cut(strip) for strip in strips]
    pivots = [jnp.zeros((SUB, BW), jnp.float32) for _ in range(groups)]
    for start in range(0, NB, INNER_NB):
        end = start + INNER_NB
        columns = {
            j: {g: jnp.broadcast_to(block[g][:, j : j + 1], (SUB, BW)) for g in range(j // SUB, groups)}
            for j in range(start, end)
        }
        for i in range(start, end):
            group, at = divmod(i, SUB)
            pivot = columns[i][group][at : at + 1, :]
            pivots[group] = jnp.where(rows == at, pivot, pivots[group])
            if i < NB - 1:
                inverse = 1.0 / pivot
                factor = {g: columns[i][g] * inverse for g in range(group, groups)}
                for j in range(i + 1, end):
                    multiple = columns[i][j // SUB][j % SUB : j % SUB + 1, :]
                    for g in range(j // SUB, groups):
                        columns[j][g] = columns[j][g] - factor[g] * multiple
                factor[group] = jnp.where(rows > at, factor[group], 0.0)
                below = range((i + 1) // SUB, groups)
                for strip in strips:
                    line = strip[group][at : at + 1, :]
                    for g in below:
                        strip[g] = strip[g] - factor[g] * line
                if end < NB:
                    line = block[group][at : at + 1, :]
                    for g in below:
                        block[g] = block[g] - factor[g][:, :NB] * line
            yield None
    scale = [lax.rsqrt(pivot) for pivot in pivots]
    yield [jnp.concatenate([x * y for x, y in zip(strip, scale)], axis=0) for strip in strips]


def side_by_side(chains):
    results = [None] * len(chains)
    for step in range(NB + 1):
        for index, chain in enumerate(chains):
            results[index] = next(chain)
    return results


def solve(gram_ref, basis_ref, rest_ref, factor_ref):
    gram = gram_ref[...]
    rest_ref[...] = product(gram, gram, 1, 0)
    panels = N // NB
    freed = last = None
    for panel in range(panels + LAG):
        chains = []
        start, behind = panel * NB, panel - LAG
        first = BW if start >= BW else 0
        if panel < panels:
            strip = rest_ref[start : start + NB, first:]
            block = strip[:, start - first : start - first + NB]
            chains.append(eliminate(block, [strip[:, c : c + BW] for c in range(0, N - first, BW)]))
        if behind >= 0:
            strip = freed
            block = product(strip, strip, 1, 1)
            if behind > 0:
                share = product(strip, last, 1, 1)
                block = block - product(share, share, 1, 1)
                strip = strip - product(share, last, 1, 0)
            chains.append(eliminate(block, [strip[:, :BW], strip[:, BW:]]))
        if 0 <= behind + 1 < panels:
            freed = factor_ref[(behind + 1) * NB : (behind + 2) * NB, :]
            if behind > 0:
                earlier = basis_ref[: behind * NB, :]
                freed = freed - product(product(freed, earlier, 1, 1), earlier, 1, 0)
        results = side_by_side(chains)
        if behind >= 0:
            last = jnp.concatenate(results[-1], axis=1)
            basis_ref[behind * NB : (behind + 1) * NB, :] = last
        if panel < panels:
            strip = jnp.concatenate(results[0], axis=1) if first == 0 else results[0][0]
            after = start + NB
            for low, high in ((after, after + NB), (after + NB, N)):
                if low < min(high, N):
                    rest_ref[low:high, first:] -= product(strip[:, low - first : high - first], strip, 0, 0)
            row = lax.broadcasted_iota(jnp.int32, strip.shape, 0) + start
            column = lax.broadcasted_iota(jnp.int32, strip.shape, 1) + first
            strip = jnp.where(column >= row, strip, 0.0)
            strip = strip if first == 0 else jnp.concatenate([jnp.zeros_like(strip), strip], axis=1)
            factor_ref[start : start + NB, :] = strip


def places(chips):
    pair, row = lax.axis_index("pair"), lax.axis_index("row")
    depth = chips // 2
    chip = lax.div(row, 2)
    return pair, row, lax.rem(row, 2), lax.div(chip, depth), lax.rem(chip, depth)


def greet(pairs, chips):
    pair, row, core, _, _ = places(chips)
    chip = lax.div(row, 2)
    barrier = pltpu.get_barrier_semaphore()

    def call(to_pair, to_row):
        pl.semaphore_signal(barrier, inc=1, device_id=(to_pair, to_row), device_id_type=MESH)

    @pl.when(pair > 0)
    def _():
        call(pair - 1, row)

    @pl.when(pair < pairs - 1)
    def _():
        call(pair + 1, row)

    for flip in (1, 2, 3):
        call(pair, quad_row(chips, flip))

    @pl.loop(1, chips)
    def _(step):
        @pl.when(step != chips // 2)
        def _():
            call(pair, lax.rem(chip + step, chips) * 2 + core)

    neighbours = jnp.where(pair > 0, 1, 0) + jnp.where(pair < pairs - 1, 1, 0)
    return lambda: pl.semaphore_wait(barrier, neighbours + 3 + chips - 2)


def quad_row(chips, flip):
    _, _, core, y, z = places(chips)
    to_core = 1 - core if flip & 1 else core
    to_y = 1 - y if flip & 2 else y
    return (to_y * (chips // 2) + z) * 2 + to_core


def copy_to(src, dst, send_sem, recv_sem, pair, row):
    return pltpu.make_async_remote_copy(
        src_ref=src, dst_ref=dst, send_sem=send_sem, recv_sem=recv_sem,
        device_id=(pair, row), device_id_type=MESH)


def wait_bytes(ref, sem):
    pltpu.make_async_copy(ref, ref, sem).wait()


def sum_all(chips, part_ref, total_ref, half_ref, slots_ref, sems, beside):
    pair, row, core, _, _ = places(chips)
    chip = lax.div(row, 2)
    piece = BW // chips
    mine = pl.multiple_of(core * BW, BW)
    theirs = pl.multiple_of(BW - core * BW, BW)
    twin = row + 1 - 2 * core

    swap = copy_to(part_ref.at[pl.ds(theirs, BW)], half_ref, sems.at[0], sems.at[1], pair, twin)
    swap.start()
    swap.wait()
    half_ref[...] += part_ref[pl.ds(mine, BW), :]

    @pl.loop(1, chips)
    def _(step):
        to = lax.rem(chip + step, chips)
        copy_to(half_ref.at[pl.ds(pl.multiple_of(to * piece, piece), piece)], slots_ref.at[step - 1],
                sems.at[2], sems.at[3], pair, to * 2 + core).start()

    beside(0)

    place = pl.multiple_of(chip * piece, piece)
    total = half_ref[pl.ds(place, piece), :]
    wait_bytes(slots_ref, sems.at[3])
    here = pl.ds(pl.multiple_of(mine + place, piece), piece)
    total_ref[here, :] = total + jnp.sum(slots_ref[...], axis=0)
    wait_bytes(slots_ref, sems.at[2])

    @pl.loop(1, chips)
    def _(step):
        to = lax.rem(chip + step, chips)
        copy_to(total_ref.at[here], total_ref.at[here], sems.at[4], sems.at[5], pair, to * 2 + core).start()

    beside(1)

    wait_bytes(slots_ref, sems.at[5])
    wait_bytes(slots_ref, sems.at[4])
    swap = copy_to(total_ref.at[pl.ds(mine, BW)], total_ref.at[pl.ds(mine, BW)], sems.at[6], sems.at[7], pair, twin)
    swap.start()
    beside(2)
    swap.wait()


def sum_cross(chips, parity, cross_ref, total_ref, near_ref, far_ref, sems, beside):
    pair, row, core, y, z = places(chips)
    depth = chips // 2
    quarter = BW // 4

    def of(to_core, to_y):
        return pl.ds(pl.multiple_of((to_core * 2 + to_y) * quarter, quarter), quarter)

    def others(src, dst, send, recv):
        return [copy_to(src(flip), dst(flip), send.at[flip - 1], recv.at[flip - 1], pair, quad_row(chips, flip))
                for flip in (1, 2, 3)]

    def theirs(flip):
        return cross_ref.at[of(1 - core if flip & 1 else core, 1 - y if flip & 2 else y)]

    copies = others(theirs, lambda flip: near_ref.at[flip - 1], sems.at[0], sems.at[1])
    for copy in copies:
        copy.start()
    beside(0)
    for copy in copies:
        copy.wait_recv()
    mine = far_ref.at[parity, z]
    mine[...] = (cross_ref[of(core, y), :] + near_ref[0]) + (near_ref[1] + near_ref[2])

    @pl.loop(1, depth)
    def _(step):
        to = (y * depth + lax.rem(z + step, depth)) * 2 + core
        copy_to(mine, mine, sems.at[2, parity], sems.at[3, parity], pair, to).start()

    beside(1)

    for copy in copies:
        copy.wait_send()
    others_far = far_ref.at[parity, pl.ds(0, depth - 1)]
    wait_bytes(others_far, sems.at[3, parity])
    total_ref[of(core, y), :] = jnp.sum(far_ref[parity], axis=0)
    here = total_ref.at[of(core, y)]
    copies = others(lambda flip: here, lambda flip: here, sems.at[4], sems.at[5])
    for copy in copies:
        copy.start()
    beside(2)
    wait_bytes(others_far, sems.at[2, parity])
    for copy in copies:
        copy.wait_recv()
    for copy in copies:
        copy.wait_send()


def rounds_kernel(pairs, chips, x_ref, out_ref, blocks_ref, gram_ref, part_ref, half_ref, slots_ref, basis_ref,
                  rest_ref, factor_ref, turn_ref, right_ref, left_ref, cross_ref, total_ref, near_ref, far_ref,
                  square_ref, square_in_ref, ahead_ref, basis_in_ref, load_sem, all_sems, cross_sems, pair_sems,
                  square_sems, ahead_sems, basis_sems):
    pair, row, _, _, _ = places(chips)
    pieces = out_ref.shape[0] // STEP
    is_first, is_last = pair == 0, pair == pairs - 1

    def window(step):
        return pl.ds(pl.multiple_of(step * STEP, STEP), STEP)

    def both_ways(left, right):
        @pl.when(pair > 0)
        def _():
            left()

        @pl.when(pair < pairs - 1)
        def _():
            right()

    def ahead_right(parity, step):
        return copy_to(blocks_ref.at[parity, window(step)], ahead_ref.at[parity, 0, window(step)],
                       ahead_sems.at[parity, 0, step], ahead_sems.at[parity, 1, step], pair + 1, row)

    def ahead_left(parity, step):
        return copy_to(blocks_ref.at[parity, window(step)], ahead_ref.at[parity, 1, window(step)],
                       ahead_sems.at[parity, 2, step], ahead_sems.at[parity, 3, step], pair - 1, row)

    def send_ahead(parity, low, high):
        @pl.loop(low, high)
        def _(step):
            both_ways(lambda: ahead_left(parity, step).start(), lambda: ahead_right(parity, step).start())

    def beside(parity):
        return lambda stage: send_ahead(parity, MARKS[stage - 1] if stage else 0, MARKS[stage])

    load = pltpu.make_async_copy(x_ref, blocks_ref.at[0], load_sem)
    load.start()
    arrive = greet(pairs, chips)
    part_ref[...] = jnp.zeros_like(part_ref)
    load.wait()

    @pl.loop(0, pieces)
    def _(step):
        block = blocks_ref[0, window(step), :]
        part_ref[...] += product(block, block, 0, 0)

    arrive()
    sum_all(chips, part_ref, gram_ref, half_ref, slots_ref, all_sems, beside(0))

    @pl.loop(0, ROUNDS)
    def _(turn):
        parity = lax.rem(turn, 2)
        later = 1 - parity
        old, new = blocks_ref.at[parity], blocks_ref.at[later]

        def to_right(step):
            return copy_to(right_ref.at[window(step - AHEAD)], new.at[window(step), pl.ds(0, BW)],
                           pair_sems.at[parity, 0, step], pair_sems.at[parity, 1, step], pair + 1, row)

        def to_left(step):
            return copy_to(left_ref.at[window(step - AHEAD)], new.at[window(step), pl.ds(BW, BW)],
                           pair_sems.at[parity, 2, step], pair_sems.at[parity, 3, step], pair - 1, row)

        def square_right():
            return copy_to(square_ref.at[0], square_in_ref.at[parity, 0],
                           square_sems.at[parity, 0], square_sems.at[parity, 1], pair + 1, row)

        def square_left():
            return copy_to(square_ref.at[1], square_in_ref.at[parity, 1],
                           square_sems.at[parity, 2], square_sems.at[parity, 3], pair - 1, row)

        def basis_right():
            start = pl.multiple_of(jnp.where(is_first, BW, 0), BW)
            return copy_to(basis_ref.at[pl.ds(start, BW)], basis_in_ref.at[parity, 0],
                           basis_sems.at[parity, 0], basis_sems.at[parity, 1], pair + 1, row)

        def basis_left():
            return copy_to(basis_ref.at[pl.ds(BW, BW)], basis_in_ref.at[parity, 1],
                           basis_sems.at[parity, 2], basis_sems.at[parity, 3], pair - 1, row)

        send_ahead(parity, MARKS[2], AHEAD)
        solve(gram_ref, basis_ref, rest_ref, factor_ref)

        @pl.loop(0, AHEAD)
        def _(step):
            both_ways(lambda: ahead_left(parity, step).wait_send(), lambda: ahead_right(parity, step).wait_send())

        both_ways(lambda: basis_left().start(), lambda: basis_right().start())
        turn_ref[...] = basis_ref[...].T

        @pl.when(is_first | is_last)
        def _():
            @pl.loop(0, pieces)
            def _(step):
                top = product(old[window(step), :], turn_ref[:, :BW], 1, 0)

                @pl.when(is_first)
                def _():
                    new[window(step), pl.ds(0, BW)] = top

                @pl.when(is_last)
                def _():
                    new[window(step), pl.ds(BW, BW)] = top

        @pl.loop(AHEAD, pieces)
        def _(step):
            turned = product(old[window(step), :], turn_ref[...], 1, 0)
            top, low = turned[:, :BW], turned[:, BW:]
            left_ref[window(step - AHEAD), :] = low
            right_ref[window(step - AHEAD), :] = jnp.where(is_first, low, top)
            both_ways(lambda: to_left(step).start(), lambda: to_right(step).start())

        top_rows, low_rows = basis_ref[:BW, :], basis_ref[BW:, :]
        top_square = product(product(top_rows, gram_ref[...], 1, 0), top_rows, 1, 1)
        low_square = product(product(low_rows, gram_ref[...], 1, 0), low_rows, 1, 1)
        square_ref[0] = jnp.where(is_first, low_square, top_square)
        square_ref[1] = low_square
        both_ways(lambda: square_left().start(), lambda: square_right().start())

        @pl.when(is_first)
        def _():
            square_in_ref[parity, 0] = top_square

        @pl.when(is_last)
        def _():
            square_in_ref[parity, 1] = top_square

        both_ways(lambda: basis_right().wait_recv(), lambda: basis_left().wait_recv())
        cross_ref[...] = jnp.zeros_like(cross_ref)

        def add_cross(step):
            block = new[window(step), :]
            cross_ref[...] += product(block[:, :BW], block[:, BW:], 0, 0)

        @pl.when(pair > 0)
        def _():
            turn_ref[:, :BW] = basis_in_ref[parity, 0].T

        @pl.when(pair < pairs - 1)
        def _():
            turn_ref[:, BW:] = basis_in_ref[parity, 1].T

        @pl.loop(0, AHEAD)
        def _(step):
            @pl.when(pair > 0)
            def _():
                ahead_right(parity, step).wait_recv()
                new[window(step), pl.ds(0, BW)] = product(
                    ahead_ref[parity, 0, window(step), :], turn_ref[:, :BW], 1, 0)

            @pl.when(pair < pairs - 1)
            def _():
                ahead_left(parity, step).wait_recv()
                new[window(step), pl.ds(BW, BW)] = product(
                    ahead_ref[parity, 1, window(step), :], turn_ref[:, BW:], 1, 0)

            add_cross(step)

        @pl.loop(AHEAD, pieces)
        def _(step):
            both_ways(lambda: to_right(step).wait_recv(), lambda: to_left(step).wait_recv())
            add_cross(step)

        @pl.when(turn < ROUNDS - 1)
        def _():
            sum_cross(chips, parity, cross_ref, total_ref, near_ref, far_ref, cross_sems, beside(later))

        both_ways(lambda: square_right().wait_recv(), lambda: square_left().wait_recv())
        both_ways(lambda: square_left().wait_send(), lambda: square_right().wait_send())
        both_ways(lambda: basis_left().wait_send(), lambda: basis_right().wait_send())
        total = total_ref[...]
        gram_ref[:BW, :BW] = square_in_ref[parity, 0]
        gram_ref[:BW, BW:] = total
        gram_ref[BW:, :BW] = total.T
        gram_ref[BW:, BW:] = square_in_ref[parity, 1]

        @pl.loop(AHEAD, pieces)
        def _(step):
            both_ways(lambda: to_left(step).wait_send(), lambda: to_right(step).wait_send())

    out_ref[...] = blocks_ref[ROUNDS % 2]


def body(pairs, chips, x):
    rows = x.shape[0]
    depth, pieces = chips // 2, rows // STEP
    f32 = jnp.float32
    square = pltpu.VMEM((N, N), f32)
    tile = pltpu.VMEM((BW, BW), f32)
    dma = pltpu.SemaphoreType.DMA
    return pl.pallas_call(
        functools.partial(rounds_kernel, pairs, chips),
        out_shape=jax.ShapeDtypeStruct(x.shape, f32),
        in_specs=[pl.BlockSpec(memory_space=pl.ANY)],
        out_specs=VMEM,
        scratch_shapes=[
            pltpu.VMEM((2, rows, N), f32),
            square,
            square,
            pltpu.VMEM((BW, N), f32),
            pltpu.VMEM((chips - 1, BW // chips, N), f32),
            square,
            square,
            square,
            square,
            pltpu.VMEM((rows - AHEAD * STEP, BW), f32),
            pltpu.VMEM((rows - AHEAD * STEP, BW), f32),
            tile,
            tile,
            pltpu.VMEM((3, BW // 4, BW), f32),
            pltpu.VMEM((2, depth, BW // 4, BW), f32),
            pltpu.VMEM((2, BW, BW), f32),
            pltpu.VMEM((2, 2, BW, BW), f32),
            pltpu.VMEM((2, 2, AHEAD * STEP, N), f32),
            pltpu.VMEM((2, 2, BW, N), f32),
            dma,
            dma((8,)),
            dma((6, 3)),
            dma((2, 4, pieces)),
            dma((2, 4)),
            dma((2, 4, pieces)),
            dma((2, 4)),
        ],
        compiler_params=pltpu.CompilerParams(
            collective_id=0, has_side_effects=True, vmem_limit_bytes=32 * 2**20
        ),
        name="rounds",
    )(x)


def solution(mesh):
    return jax.shard_map(
        functools.partial(body, mesh.shape["pair"], mesh.shape["row"] // 2),
        mesh=mesh,
        in_specs=(P("row", "pair"),),
        out_specs=P("row", "pair"),
        check_vma=False,
    )
```

```python
import functools

import jax
import jax.numpy as jnp
from jax import lax
from jax.experimental import pallas as pl
from jax.experimental.pallas import tpu as pltpu
from jax.sharding import PartitionSpec as P

ROUNDS = 3
BW = 128
N = 2 * BW
NB = 32
INNER_NB = 16
SUB = 8
LAG = 2
STEP = 256
AHEAD = 2
MARKS = (0, 0, 1)
MESH = pl.DeviceIdType.MESH
HIGHEST = lax.Precision.HIGHEST
VMEM = pl.BlockSpec(memory_space=pltpu.VMEM)


def product(a, b, a_dim, b_dim):
    dims = (((a_dim,), (b_dim,)), ((), ()))
    return lax.dot_general(a, b, dims, precision=HIGHEST, preferred_element_type=jnp.float32)


def eliminate(block, strips):
    groups = NB // SUB
    rows = lax.broadcasted_iota(jnp.int32, (SUB, BW), 0)

    def cut(array):
        return [array[group * SUB : (group + 1) * SUB, :] for group in range(groups)]

    block, strips = cut(block), [cut(strip) for strip in strips]
    pivots = [jnp.zeros((SUB, BW), jnp.float32) for _ in range(groups)]
    for start in range(0, NB, INNER_NB):
        end = start + INNER_NB
        columns = {
            j: {g: jnp.broadcast_to(block[g][:, j : j + 1], (SUB, BW)) for g in range(j // SUB, groups)}
            for j in range(start, end)
        }
        for i in range(start, end):
            group, at = divmod(i, SUB)
            pivot = columns[i][group][at : at + 1, :]
            pivots[group] = jnp.where(rows == at, pivot, pivots[group])
            if i < NB - 1:
                inverse = 1.0 / pivot
                factor = {g: columns[i][g] * inverse for g in range(group, groups)}
                for j in range(i + 1, end):
                    multiple = columns[i][j // SUB][j % SUB : j % SUB + 1, :]
                    for g in range(j // SUB, groups):
                        columns[j][g] = columns[j][g] - factor[g] * multiple
                factor[group] = jnp.where(rows > at, factor[group], 0.0)
                below = range((i + 1) // SUB, groups)
                for strip in strips:
                    line = strip[group][at : at + 1, :]
                    for g in below:
                        strip[g] = strip[g] - factor[g] * line
                if end < NB:
                    line = block[group][at : at + 1, :]
                    for g in below:
                        block[g] = block[g] - factor[g][:, :NB] * line
            yield None
    scale = [lax.rsqrt(pivot) for pivot in pivots]
    yield [jnp.concatenate([x * y for x, y in zip(strip, scale)], axis=0) for strip in strips]


def side_by_side(chains):
    results = [None] * len(chains)
    for step in range(NB + 1):
        for index, chain in enumerate(chains):
            results[index] = next(chain)
    return results


def solve(gram_ref, basis_ref, rest_ref, factor_ref):
    gram = gram_ref[...]
    rest_ref[...] = product(gram, gram, 1, 0)
    panels = N // NB
    freed = last = None
    for panel in range(panels + LAG):
        chains = []
        start, behind = panel * NB, panel - LAG
        first = BW if start >= BW else 0
        if panel < panels:
            strip = rest_ref[start : start + NB, first:]
            block = strip[:, start - first : start - first + NB]
            chains.append(eliminate(block, [strip[:, c : c + BW] for c in range(0, N - first, BW)]))
        if behind >= 0:
            strip = freed
            block = product(strip, strip, 1, 1)
            if behind > 0:
                share = product(strip, last, 1, 1)
                block = block - product(share, share, 1, 1)
                strip = strip - product(share, last, 1, 0)
            chains.append(eliminate(block, [strip[:, :BW], strip[:, BW:]]))
        if 0 <= behind + 1 < panels:
            freed = factor_ref[(behind + 1) * NB : (behind + 2) * NB, :]
            if behind > 0:
                earlier = basis_ref[: behind * NB, :]
                freed = freed - product(product(freed, earlier, 1, 1), earlier, 1, 0)
        results = side_by_side(chains)
        if behind >= 0:
            last = jnp.concatenate(results[-1], axis=1)
            basis_ref[behind * NB : (behind + 1) * NB, :] = last
        if panel < panels:
            strip = jnp.concatenate(results[0], axis=1) if first == 0 else results[0][0]
            after = start + NB
            for low, high in ((after, after + NB), (after + NB, N)):
                if low < min(high, N):
                    rest_ref[low:high, first:] -= product(strip[:, low - first : high - first], strip, 0, 0)
            row = lax.broadcasted_iota(jnp.int32, strip.shape, 0) + start
            column = lax.broadcasted_iota(jnp.int32, strip.shape, 1) + first
            strip = jnp.where(column >= row, strip, 0.0)
            strip = strip if first == 0 else jnp.concatenate([jnp.zeros_like(strip), strip], axis=1)
            factor_ref[start : start + NB, :] = strip


def places(chips):
    pair, row = lax.axis_index("pair"), lax.axis_index("row")
    depth = chips // 2
    chip = lax.div(row, 2)
    return pair, row, lax.rem(row, 2), lax.div(chip, depth), lax.rem(chip, depth)


def greet(pairs, chips):
    pair, row, core, _, _ = places(chips)
    chip = lax.div(row, 2)
    barrier = pltpu.get_barrier_semaphore()

    def call(to_pair, to_row):
        pl.semaphore_signal(barrier, inc=1, device_id=(to_pair, to_row), device_id_type=MESH)

    @pl.when(pair > 0)
    def _():
        call(pair - 1, row)

    @pl.when(pair < pairs - 1)
    def _():
        call(pair + 1, row)

    for flip in (1, 2, 3):
        call(pair, quad_row(chips, flip))

    @pl.loop(1, chips)
    def _(step):
        @pl.when(step != chips // 2)
        def _():
            call(pair, lax.rem(chip + step, chips) * 2 + core)

    neighbours = jnp.where(pair > 0, 1, 0) + jnp.where(pair < pairs - 1, 1, 0)
    return lambda: pl.semaphore_wait(barrier, neighbours + 3 + chips - 2)


def quad_row(chips, flip):
    _, _, core, y, z = places(chips)
    to_core = 1 - core if flip & 1 else core
    to_y = 1 - y if flip & 2 else y
    return (to_y * (chips // 2) + z) * 2 + to_core


def copy_to(src, dst, send_sem, recv_sem, pair, row):
    return pltpu.make_async_remote_copy(
        src_ref=src, dst_ref=dst, send_sem=send_sem, recv_sem=recv_sem,
        device_id=(pair, row), device_id_type=MESH)


def wait_bytes(ref, sem):
    pltpu.make_async_copy(ref, ref, sem).wait()


def sum_all(chips, part_ref, total_ref, half_ref, slots_ref, sems, beside):
    pair, row, core, _, _ = places(chips)
    chip = lax.div(row, 2)
    piece = BW // chips
    mine = pl.multiple_of(core * BW, BW)
    theirs = pl.multiple_of(BW - core * BW, BW)
    twin = row + 1 - 2 * core

    swap = copy_to(part_ref.at[pl.ds(theirs, BW)], half_ref, sems.at[0], sems.at[1], pair, twin)
    swap.start()
    swap.wait()
    half_ref[...] += part_ref[pl.ds(mine, BW), :]

    @pl.loop(1, chips)
    def _(step):
        to = lax.rem(chip + step, chips)
        copy_to(half_ref.at[pl.ds(pl.multiple_of(to * piece, piece), piece)], slots_ref.at[step - 1],
                sems.at[2], sems.at[3], pair, to * 2 + core).start()

    beside(0)

    place = pl.multiple_of(chip * piece, piece)
    total = half_ref[pl.ds(place, piece), :]
    wait_bytes(slots_ref, sems.at[3])
    here = pl.ds(pl.multiple_of(mine + place, piece), piece)
    total_ref[here, :] = total + jnp.sum(slots_ref[...], axis=0)
    wait_bytes(slots_ref, sems.at[2])

    @pl.loop(1, chips)
    def _(step):
        to = lax.rem(chip + step, chips)
        copy_to(total_ref.at[here], total_ref.at[here], sems.at[4], sems.at[5], pair, to * 2 + core).start()

    beside(1)

    wait_bytes(slots_ref, sems.at[5])
    wait_bytes(slots_ref, sems.at[4])
    swap = copy_to(total_ref.at[pl.ds(mine, BW)], total_ref.at[pl.ds(mine, BW)], sems.at[6], sems.at[7], pair, twin)
    swap.start()
    beside(2)
    swap.wait()


def sum_cross(chips, parity, cross_ref, total_ref, near_ref, far_ref, sems, beside):
    pair, row, core, y, z = places(chips)
    depth = chips // 2
    quarter = BW // 4

    def of(to_core, to_y):
        return pl.ds(pl.multiple_of((to_core * 2 + to_y) * quarter, quarter), quarter)

    def others(src, dst, send, recv):
        return [copy_to(src(flip), dst(flip), send.at[flip - 1], recv.at[flip - 1], pair, quad_row(chips, flip))
                for flip in (1, 2, 3)]

    def theirs(flip):
        return cross_ref.at[of(1 - core if flip & 1 else core, 1 - y if flip & 2 else y)]

    copies = others(theirs, lambda flip: near_ref.at[flip - 1], sems.at[0], sems.at[1])
    for copy in copies:
        copy.start()
    beside(0)
    for copy in copies:
        copy.wait_recv()
    mine = far_ref.at[parity, z]
    mine[...] = (cross_ref[of(core, y), :] + near_ref[0]) + (near_ref[1] + near_ref[2])

    @pl.loop(1, depth)
    def _(step):
        to = (y * depth + lax.rem(z + step, depth)) * 2 + core
        copy_to(mine, mine, sems.at[2, parity], sems.at[3, parity], pair, to).start()

    beside(1)

    for copy in copies:
        copy.wait_send()
    others_far = far_ref.at[parity, pl.ds(0, depth - 1)]
    wait_bytes(others_far, sems.at[3, parity])
    total_ref[of(core, y), :] = jnp.sum(far_ref[parity], axis=0)
    here = total_ref.at[of(core, y)]
    copies = others(lambda flip: here, lambda flip: here, sems.at[4], sems.at[5])
    for copy in copies:
        copy.start()
    beside(2)
    wait_bytes(others_far, sems.at[2, parity])
    for copy in copies:
        copy.wait_recv()
    for copy in copies:
        copy.wait_send()


def rounds_kernel(pairs, chips, x_ref, out_ref, blocks_ref, gram_ref, part_ref, half_ref, slots_ref, basis_ref,
                  rest_ref, factor_ref, turn_ref, right_ref, left_ref, cross_ref, total_ref, near_ref, far_ref,
                  square_ref, square_in_ref, ahead_ref, basis_in_ref, load_sem, all_sems, cross_sems, pair_sems,
                  square_sems, ahead_sems, basis_sems):
    pair, row, _, _, _ = places(chips)
    pieces = out_ref.shape[0] // STEP
    is_first, is_last = pair == 0, pair == pairs - 1

    def window(step):
        return pl.ds(pl.multiple_of(step * STEP, STEP), STEP)

    def both_ways(left, right):
        @pl.when(pair > 0)
        def _():
            left()

        @pl.when(pair < pairs - 1)
        def _():
            right()

    def ahead_right(parity, step):
        return copy_to(blocks_ref.at[parity, window(step)], ahead_ref.at[parity, 0, window(step)],
                       ahead_sems.at[parity, 0, step], ahead_sems.at[parity, 1, step], pair + 1, row)

    def ahead_left(parity, step):
        return copy_to(blocks_ref.at[parity, window(step)], ahead_ref.at[parity, 1, window(step)],
                       ahead_sems.at[parity, 2, step], ahead_sems.at[parity, 3, step], pair - 1, row)

    def send_ahead(parity, low, high):
        @pl.loop(low, high)
        def _(step):
            both_ways(lambda: ahead_left(parity, step).start(), lambda: ahead_right(parity, step).start())

    def beside(parity):
        return lambda stage: send_ahead(parity, MARKS[stage - 1] if stage else 0, MARKS[stage])

    load = pltpu.make_async_copy(x_ref, blocks_ref.at[0], load_sem)
    load.start()
    arrive = greet(pairs, chips)
    part_ref[...] = jnp.zeros_like(part_ref)
    load.wait()

    @pl.loop(0, pieces)
    def _(step):
        block = blocks_ref[0, window(step), :]
        part_ref[...] += product(block, block, 0, 0)

    arrive()
    sum_all(chips, part_ref, gram_ref, half_ref, slots_ref, all_sems, beside(0))

    @pl.loop(0, ROUNDS)
    def _(turn):
        parity = lax.rem(turn, 2)
        later = 1 - parity
        old, new = blocks_ref.at[parity], blocks_ref.at[later]

        def to_right(step):
            return copy_to(right_ref.at[window(step - AHEAD)], new.at[window(step), pl.ds(0, BW)],
                           pair_sems.at[parity, 0, step], pair_sems.at[parity, 1, step], pair + 1, row)

        def to_left(step):
            return copy_to(left_ref.at[window(step - AHEAD)], new.at[window(step), pl.ds(BW, BW)],
                           pair_sems.at[parity, 2, step], pair_sems.at[parity, 3, step], pair - 1, row)

        def square_right():
            return copy_to(square_ref.at[0], square_in_ref.at[parity, 0],
                           square_sems.at[parity, 0], square_sems.at[parity, 1], pair + 1, row)

        def square_left():
            return copy_to(square_ref.at[1], square_in_ref.at[parity, 1],
                           square_sems.at[parity, 2], square_sems.at[parity, 3], pair - 1, row)

        def basis_right():
            start = pl.multiple_of(jnp.where(is_first, BW, 0), BW)
            return copy_to(basis_ref.at[pl.ds(start, BW)], basis_in_ref.at[parity, 0],
                           basis_sems.at[parity, 0], basis_sems.at[parity, 1], pair + 1, row)

        def basis_left():
            return copy_to(basis_ref.at[pl.ds(BW, BW)], basis_in_ref.at[parity, 1],
                           basis_sems.at[parity, 2], basis_sems.at[parity, 3], pair - 1, row)

        send_ahead(parity, MARKS[2], AHEAD)
        solve(gram_ref, basis_ref, rest_ref, factor_ref)

        @pl.loop(0, AHEAD)
        def _(step):
            both_ways(lambda: ahead_left(parity, step).wait_send(), lambda: ahead_right(parity, step).wait_send())

        both_ways(lambda: basis_left().start(), lambda: basis_right().start())
        turn_ref[...] = basis_ref[...].T

        @pl.when(is_first | is_last)
        def _():
            @pl.loop(0, pieces)
            def _(step):
                top = product(old[window(step), :], turn_ref[:, :BW], 1, 0)

                @pl.when(is_first)
                def _():
                    new[window(step), pl.ds(0, BW)] = top

                @pl.when(is_last)
                def _():
                    new[window(step), pl.ds(BW, BW)] = top

        @pl.loop(AHEAD, pieces)
        def _(step):
            turned = product(old[window(step), :], turn_ref[...], 1, 0)
            top, low = turned[:, :BW], turned[:, BW:]
            left_ref[window(step - AHEAD), :] = low
            right_ref[window(step - AHEAD), :] = jnp.where(is_first, low, top)
            both_ways(lambda: to_left(step).start(), lambda: to_right(step).start())

        top_rows, low_rows = basis_ref[:BW, :], basis_ref[BW:, :]
        top_square = product(product(top_rows, gram_ref[...], 1, 0), top_rows, 1, 1)
        low_square = product(product(low_rows, gram_ref[...], 1, 0), low_rows, 1, 1)
        square_ref[0] = jnp.where(is_first, low_square, top_square)
        square_ref[1] = low_square
        both_ways(lambda: square_left().start(), lambda: square_right().start())

        @pl.when(is_first)
        def _():
            square_in_ref[parity, 0] = top_square

        @pl.when(is_last)
        def _():
            square_in_ref[parity, 1] = top_square

        both_ways(lambda: basis_right().wait_recv(), lambda: basis_left().wait_recv())
        cross_ref[...] = jnp.zeros_like(cross_ref)

        def add_cross(step):
            block = new[window(step), :]
            cross_ref[...] += product(block[:, :BW], block[:, BW:], 0, 0)

        @pl.when(pair > 0)
        def _():
            turn_ref[:, :BW] = basis_in_ref[parity, 0].T

        @pl.when(pair < pairs - 1)
        def _():
            turn_ref[:, BW:] = basis_in_ref[parity, 1].T

        @pl.loop(0, AHEAD)
        def _(step):
            @pl.when(pair > 0)
            def _():
                ahead_right(parity, step).wait_recv()
                new[window(step), pl.ds(0, BW)] = product(
                    ahead_ref[parity, 0, window(step), :], turn_ref[:, :BW], 1, 0)

            @pl.when(pair < pairs - 1)
            def _():
                ahead_left(parity, step).wait_recv()
                new[window(step), pl.ds(BW, BW)] = product(
                    ahead_ref[parity, 1, window(step), :], turn_ref[:, BW:], 1, 0)

            add_cross(step)

        @pl.loop(AHEAD, pieces)
        def _(step):
            both_ways(lambda: to_right(step).wait_recv(), lambda: to_left(step).wait_recv())
            add_cross(step)

        @pl.when(turn < ROUNDS - 1)
        def _():
            sum_cross(chips, parity, cross_ref, total_ref, near_ref, far_ref, cross_sems, beside(later))

        both_ways(lambda: square_right().wait_recv(), lambda: square_left().wait_recv())
        both_ways(lambda: square_left().wait_send(), lambda: square_right().wait_send())
        both_ways(lambda: basis_left().wait_send(), lambda: basis_right().wait_send())
        total = total_ref[...]
        gram_ref[:BW, :BW] = square_in_ref[parity, 0]
        gram_ref[:BW, BW:] = total
        gram_ref[BW:, :BW] = total.T
        gram_ref[BW:, BW:] = square_in_ref[parity, 1]

        @pl.loop(AHEAD, pieces)
        def _(step):
            both_ways(lambda: to_left(step).wait_send(), lambda: to_right(step).wait_send())

    out_ref[...] = blocks_ref[ROUNDS % 2]


def body(pairs, chips, x):
    rows = x.shape[0]
    depth, pieces = chips // 2, rows // STEP
    f32 = jnp.float32
    square = pltpu.VMEM((N, N), f32)
    tile = pltpu.VMEM((BW, BW), f32)
    dma = pltpu.SemaphoreType.DMA
    return pl.pallas_call(
        functools.partial(rounds_kernel, pairs, chips),
        out_shape=jax.ShapeDtypeStruct(x.shape, f32),
        in_specs=[pl.BlockSpec(memory_space=pl.ANY)],
        out_specs=VMEM,
        scratch_shapes=[
            pltpu.VMEM((2, rows, N), f32),
            square,
            square,
            pltpu.VMEM((BW, N), f32),
            pltpu.VMEM((chips - 1, BW // chips, N), f32),
            square,
            square,
            square,
            square,
            pltpu.VMEM((rows - AHEAD * STEP, BW), f32),
            pltpu.VMEM((rows - AHEAD * STEP, BW), f32),
            tile,
            tile,
            pltpu.VMEM((3, BW // 4, BW), f32),
            pltpu.VMEM((2, depth, BW // 4, BW), f32),
            pltpu.VMEM((2, BW, BW), f32),
            pltpu.VMEM((2, 2, BW, BW), f32),
            pltpu.VMEM((2, 2, AHEAD * STEP, N), f32),
            pltpu.VMEM((2, 2, BW, N), f32),
            dma,
            dma((8,)),
            dma((6, 3)),
            dma((2, 4, pieces)),
            dma((2, 4)),
            dma((2, 4, pieces)),
            dma((2, 4)),
        ],
        compiler_params=pltpu.CompilerParams(
            collective_id=0, has_side_effects=True, vmem_limit_bytes=32 * 2**20
        ),
        name="rounds",
    )(x)


def solution(mesh):
    return jax.shard_map(
        functools.partial(body, mesh.shape["pair"], mesh.shape["row"] // 2),
        mesh=mesh,
        in_specs=(P("row", "pair"),),
        out_specs=P("row", "pair"),
        check_vma=False,
    )
```
